32 devices in a mesh: prow: 8 (over z, y), pcol: 4 (over x, core).
Axes of the slice: x: 2, y: 2, z: 4, core: 2. Of those that a mesh axis runs over, the one named last changes fastest.
Arguments:
- panel_rows: float32 [2, 1024, 12288], P(None, None, ('prow', 'pcol')), may hold values from -0.109375 to 0.109375
- solved: float32 [12288, 1024], P(('prow', 'pcol')), may hold values from -6 to 6
- right_side: float32 [2, 1024, 1024], P(None, 'prow', 'pcol'), may hold values from -6 to 6
- coupling: float32 [1024, 1024], P(None, 'prow'), may hold values from -0.1875 to 0.1875
- inverses: float32 [2, 1024, 1024], P(None, 'prow'), may hold values from -2 to 2, as said below
Outputs:
- panels: float32 [2, 1024, 1024], P(None, 'prow', 'pcol')
The draws below stay inside these ranges and needn't reach their ends.
Inputs may be any that keep to these rules, and one draw needn't show every extreme that they name: `inverses`: each tile is zero above its diagonal, and its diagonal entries are positive.
All inputs are finite; a program needn't handle non-finite values.
Results may differ from the reference program's by a relative error of at most 0.000088.
Values sent between devices are 32-bit elements; how exact they have to be, the bound alone decides.
A program may use at most 64 MiB of HBM per device.

```python
import jax
import jax.numpy as jnp
from jax import lax

NB = 1024
RHS = 1024
SOLVED = 12288


def draw_inverses(key, part):
    keyed = jax.random.fold_in(key, 31)
    key_lower, key_diag = jax.random.split(keyed)
    reach = jnp.sqrt(3.0 / NB)
    lower_part = jax.random.uniform(key_lower, (2, NB, NB), jnp.float32, -reach, reach)
    diag_values = jax.random.uniform(key_diag, (2, NB), jnp.float32, 0.5, 1.5)
    lower_part = jnp.tril(lower_part, -1)
    identity = jnp.eye(NB, dtype=jnp.float32)
    return lower_part + diag_values[:, :, None] * identity[None, :, :]


def spiked(values, rng, source, target, shards_of, factor):
    owner, partner = [(jnp.arange(values.shape[dim]) // (values.shape[dim] // shards_of)).reshape([-1 if axis == dim else 1 for axis in range(values.ndim)]) for dim in (source, target)]
    chosen = jax.random.permutation(rng, shards_of)[partner]
    strong = (owner == chosen) | (owner == (partner + shards_of // 2) % shards_of)
    return jnp.where(strong, factor * values, values)


def block_levels(rng, extent, cuts, least, high):
    gain = 1.0
    for dim, blocks in cuts:
        draws = jax.random.uniform(jax.random.fold_in(jax.random.fold_in(rng, 6), dim), (blocks,), jnp.float32, least / len(cuts), high / len(cuts))
        gain = gain * jnp.repeat(jnp.exp(draws), extent[dim] // blocks).reshape((-1,) + (1,) * (len(extent) - 1 - dim))
    return gain


def gaussian(own_key, extent, spread, most, cuts=(), kind=jnp.bfloat16):
    entries = spread * jax.random.normal(own_key, extent, jnp.float32)
    if cuts:
        entries = entries * block_levels(own_key, extent, cuts, -0.22, 0.18)
    return jnp.clip(entries, -most, most).astype(kind)


def noise_with(key, shape, scale, bound, shards, heavy, held_as=jnp.bfloat16):
    entries = scale * jax.random.normal(key, shape, jnp.float32)
    if shards:
        entries = entries * block_levels(key, shape, shards, -0.22, 0.18)
    return jnp.clip(spiked(entries, jax.random.fold_in(key, 3), *heavy), -bound, bound).astype(held_as)


def setup_inputs(seed: int = 0) -> dict:
    seeds = jax.random.split(jax.random.key(seed), 6)
    return {
        "panel_rows": noise_with(seeds[0], (2, NB, SOLVED), SOLVED ** -0.5, 0.109375, ((2, 32),), (2, 1, 32, 2.75), jnp.float32),
        "solved": gaussian(seeds[1], (SOLVED, RHS), 1.0, 6.0, ((0, 32),), jnp.float32),
        "right_side": gaussian(seeds[2], (2, NB, RHS), 1.0, 6.0, ((1, 8), (2, 4)), jnp.float32),
        "coupling": gaussian(seeds[3], (NB, NB), NB ** -0.5, 0.1875, ((1, 8),), jnp.float32),
        "inverses": draw_inverses(jax.random.fold_in(seeds[5], 71), 0),
    }


def reference(panel_rows, solved, right_side, coupling, inverses):
    highest = lax.Precision.HIGHEST
    old_first = jnp.dot(panel_rows[0], solved, precision=highest, preferred_element_type=jnp.float32)
    old_second = jnp.dot(panel_rows[1], solved, precision=highest, preferred_element_type=jnp.float32)
    first_rest = right_side[0] - old_first
    first_panel = jnp.dot(inverses[0], first_rest, precision=highest, preferred_element_type=jnp.float32)
    coupled = jnp.dot(coupling, first_panel, precision=highest, preferred_element_type=jnp.float32)
    second_rest = right_side[1] - old_second - coupled
    second_panel = jnp.dot(inverses[1], second_rest, precision=highest, preferred_element_type=jnp.float32)
    return jnp.stack([first_panel, second_panel])
```

```python
import functools

import jax
import jax.numpy as jnp
from jax import lax
from jax.experimental import pallas as pl
from jax.experimental.pallas import tpu as pltpu
from jax.sharding import PartitionSpec as P

MESH = pl.DeviceIdType.MESH
F32 = jnp.float32
BF16 = jnp.bfloat16


def split(value):
    high = value.astype(BF16)
    return high, (value - high.astype(F32)).astype(BF16)


def product(left_high, left_low, right_high, right_low):
    dot = functools.partial(jnp.dot, preferred_element_type=F32)
    small = dot(left_low, right_high) + dot(left_high, right_low)
    return small + dot(left_high, right_high)


def kernel(
    sizes, panel, solved, right_side, coupling, inverses, out,
    left0, left1, right, inv_high, inv_low,
    send0, recv0, own0, send1, recv1, own1,
    x_first, y_first, y_second, x_second, z_last, x_one,
    gathered, coupled, y_coupled, z_coupled,
    core0_s, core0_r, core1_s, core1_r, xf_s, xf_r, yf_s, yf_r, ys_s, ys_r,
    xs_s, xs_r, zl_s, zl_r, xo_s, xo_r, gz_s, gz_r, gy_s, gy_r, yc_s, yc_r, zc_s, zc_r,
):
    A, B, X, K, tr, hr, cw = sizes
    row, col = lax.axis_index("prow"), lax.axis_index("pcol")
    a, b = row // B, row % B
    x, c = col // 2, col % 2
    other_b, other_c = 1 - b, 1 - c

    def at(a_, b_, x_, c_):
        return (a_ * B + b_, x_ * 2 + c_)

    core_peer = at(a, b, x, other_c)
    y_peer = at(a, other_b, x, c)

    def x_peer(d):
        return at(a, b, lax.rem(x + d, X), c)

    def z_peer(d):
        return at(lax.rem(a + d, A), b, x, c)

    peers = [core_peer, y_peer]
    peers += [x_peer(d) for d in range(1, X)] + [z_peer(d) for d in range(1, A)]
    barrier = pltpu.get_barrier_semaphore()
    for peer in peers:
        pl.semaphore_signal(barrier, inc=1, device_id=peer, device_id_type=MESH)

    def copy(src, dst, s, r, peer):
        return pltpu.make_async_remote_copy(
            src_ref=src, dst_ref=dst, send_sem=s, recv_sem=r,
            device_id=peer, device_id_type=MESH,
        )

    def split_right(q):
        high, low = split(solved[:, q * cw:(q + 1) * cw])
        right[q, 0:K] = high
        right[q, K:2 * K] = low
        right[q, 2 * K:] = high

    def split_left(dst, value):
        high, low = split(value)
        dst[:, 0:K] = high
        dst[:, K:2 * K] = high
        dst[:, 2 * K:] = low

    for q in range(2 * X):
        split_right(q)
    for h in range(2):
        for b_ in range(B):
            split_left(left0.at[h, b_], panel[0, :, b_, h].reshape(A * hr, K))

    pl.semaphore_wait(barrier, len(peers))

    core0, core1 = {}, {}
    for h in range(2):
        lhs = left0.at[h]

        @pl.loop(0, X)
        def _(x_):
            value = jnp.dot(lhs[...].reshape(B * A * hr, 3 * K), right[x_ * 2 + other_c], preferred_element_type=F32)
            send0[h, x_] = value.reshape(B, A, hr, cw)
            copy(send0.at[h, x_], recv0.at[h, x_], core0_s.at[h, x_], core0_r.at[h, x_], core_peer).start()

    flying = []
    for h in range(2):
        lhs = left0.at[h]

        @pl.loop(0, X)
        def _(x_):
            value = jnp.dot(lhs[...].reshape(B * A * hr, 3 * K), right[x_ * 2 + c], preferred_element_type=F32)
            copy(send0.at[h, x_], recv0.at[h, x_], core0_s.at[h, x_], core0_r.at[h, x_], core_peer).wait()
            own0[h, x_] = value.reshape(B, A, hr, cw) + recv0[h, x_]

        if h == 0:
            first = [copy(own0.at[0, lax.rem(x + d, X)], x_first.at[d - 1], xf_s.at[d - 1], xf_r.at[d - 1], x_peer(d)) for d in range(1, X)]
            for each in first:
                each.start()
        else:
            first_v = copy(own0.at[1, :, other_b], y_first, yf_s, yf_r, y_peer)
            first_v.start()

    for b_ in range(B):
        split_left(left1.at[b_], panel[1, :, b_].reshape(A * tr, K))
    for b_ in range(B):
        lhs = left1.at[b_]

        @pl.loop(0, X)
        def _(x_):
            value = jnp.dot(lhs[...], right[x_ * 2 + other_c], preferred_element_type=F32)
            send1[x_, b_] = value.reshape(A, tr, cw)
            copy(send1.at[x_, b_], recv1.at[x_, b_], core1_s.at[x_, b_], core1_r.at[x_, b_], core_peer).start()

    for b_ in range(B):
        lhs = left1.at[b_]

        @pl.loop(0, X)
        def _(x_):
            value = jnp.dot(lhs[...], right[x_ * 2 + c], preferred_element_type=F32)
            copy(send1.at[x_, b_], recv1.at[x_, b_], core1_s.at[x_, b_], core1_r.at[x_, b_], core_peer).wait()
            own1[x_, b_] = value.reshape(A, tr, cw) + recv1[x_, b_]

    for p in range(2):
        high, low = split(inverses[p])
        inv_high[p] = high
        inv_low[p] = low

    for each in first:
        each.wait()
    total = own0[0, x]
    for d in range(1, X):
        total = total + x_first[d - 1]
    own0[0, x] = total
    second = copy(own0.at[0, x, other_b], y_second, ys_s, ys_r, y_peer)
    second.start()
    first_v.wait()
    for x_ in range(X):
        own0[1, x_, b] = own0[1, x_, b] + y_first[x_]
    second_v = [copy(own0.at[1, lax.rem(x + d, X), b], x_second.at[d - 1], xs_s.at[d - 1], xs_r.at[d - 1], x_peer(d)) for d in range(1, X)]
    for each in second_v:
        each.start()
    one = [copy(own1.at[lax.rem(x + d, X)], x_one.at[d - 1], xo_s.at[d - 1], xo_r.at[d - 1], x_peer(d)) for d in range(1, X)]
    for each in one:
        each.start()

    last = []
    second.wait()
    own0[0, x, b] = own0[0, x, b] + y_second[...]
    for h in range(2):
        if h == 1:
            for each in second_v:
                each.wait()
            total = own0[1, x, b]
            for d in range(1, X):
                total = total + x_second[d - 1]
            own0[1, x, b] = total
        for d in range(1, A):
            each = copy(own0.at[h, x, b, lax.rem(a + d, A)], z_last.at[h, d - 1], zl_s.at[h, d - 1], zl_r.at[h, d - 1], z_peer(d))
            each.start()
            last.append(each)
    for each in last:
        each.wait()
    for h in range(2):
        total = own0[h, x, b, a]
        for d in range(1, A):
            total = total + z_last[h, d - 1]
        gathered[0, a, b, h * hr:(h + 1) * hr] = right_side[0, h * hr:(h + 1) * hr] - total

    def gather(p):
        shard = gathered.at[p, a, b]
        along_z = [copy(shard, shard, gz_s.at[p, d], gz_r.at[p, d], z_peer(d)) for d in range(1, A)]
        for each in along_z:
            each.start()
        along_y = [copy(shard, shard, gy_s.at[p, 0], gy_r.at[p, 0], y_peer)]
        along_y[0].start()
        for d in range(1, A):
            along_z[d - 1].wait()
            got = gathered.at[p, lax.rem(a + A - d, A), b]
            along_y.append(copy(got, got, gy_s.at[p, d], gy_r.at[p, d], y_peer))
            along_y[-1].start()
        for each in along_y:
            each.wait()
        high, low = split(gathered[p].reshape(A * B * tr, cw))
        return product(inv_high[p], inv_low[p], high, low)

    first_panel = gather(0)
    out[0] = first_panel
    panel_high, panel_low = split(first_panel)

    for each in one:
        each.wait()
    along_y, along_z = [], []

    def term(b_):
        high, low = split(coupling[:, b_].reshape(A * tr, tr))
        value = product(high, low, panel_high, panel_low).reshape(A, tr, cw) + own1[x, b_]
        for d in range(1, X):
            value = value + x_one[d - 1, b_]
        return value

    coupled[0] = term(other_b)
    for d in list(range(1, A)) + [0]:
        a_ = lax.rem(a + d, A)
        each = copy(coupled.at[0, a_], y_coupled.at[a_], yc_s.at[d], yc_r.at[d], y_peer)
        each.start()
        along_y.append(each)
    coupled[1] = term(b)
    for d in range(1, A):
        a_ = lax.rem(a + d, A)
        along_y[d - 1].wait()
        coupled[1, a_] = coupled[1, a_] + y_coupled[a_]
        each = copy(coupled.at[1, a_], z_coupled.at[d - 1], zc_s.at[d - 1], zc_r.at[d - 1], z_peer(d))
        each.start()
        along_z.append(each)
    along_y[-1].wait()
    total = coupled[1, a] + y_coupled[a]
    for d in range(1, A):
        along_z[d - 1].wait()
        total = total + z_coupled[d - 1]
    gathered[1, a, b] = right_side[1] - total
    out[1] = gather(1)


def body(R, C, panel_rows, solved, right_side, coupling, inverses):
    B = 2
    A, X = R // B, C // 2
    K = panel_rows.shape[2]
    tr, cw = right_side.shape[1:]
    hr = tr // 2
    vmem, dma = pltpu.VMEM, pltpu.SemaphoreType.DMA
    steps = [(2, X), (X, B), (max(X - 1, 1),), (), (), (max(X - 1, 1),), (2, A - 1), (X - 1,), (2, A), (2, A), (A,), (A - 1,)]
    sems = []
    for shape in steps:
        sems += [dma(shape) if shape else dma, dma(shape) if shape else dma]
    return pl.pallas_call(
        functools.partial(kernel, (A, B, X, K, tr, hr, cw)),
        out_shape=jax.ShapeDtypeStruct((2, tr, cw), F32),
        in_specs=[pl.BlockSpec(memory_space=pltpu.VMEM)] * 5,
        out_specs=pl.BlockSpec(memory_space=pltpu.VMEM),
        scratch_shapes=[
            vmem((2, B, A * hr, 3 * K), BF16),
            vmem((B, A * tr, 3 * K), BF16),
            vmem((C, 3 * K, cw), BF16),
            vmem((2, tr, R * tr), BF16),
            vmem((2, tr, R * tr), BF16),
            vmem((2, X, B, A, hr, cw), F32),
            vmem((2, X, B, A, hr, cw), F32),
            vmem((2, X, B, A, hr, cw), F32),
            vmem((X, B, A, tr, cw), F32),
            vmem((X, B, A, tr, cw), F32),
            vmem((X, B, A, tr, cw), F32),
            vmem((X - 1, B, A, hr, cw), F32),
            vmem((X, A, hr, cw), F32),
            vmem((A, hr, cw), F32),
            vmem((X - 1, A, hr, cw), F32),
            vmem((2, A - 1, hr, cw), F32),
            vmem((X - 1, B, A, tr, cw), F32),
            vmem((2, A, B, tr, cw), F32),
            vmem((2, A, tr, cw), F32),
            vmem((A, tr, cw), F32),
            vmem((A - 1, tr, cw), F32),
        ] + sems,
        compiler_params=pltpu.CompilerParams(
            collective_id=0, has_side_effects=True, vmem_limit_bytes=56 << 20
        ),
    )(
        panel_rows.reshape(2, A, B, 2, hr, K),
        solved,
        right_side,
        coupling.reshape(A, B, tr, tr),
        inverses,
    )


def solution(mesh):
    return jax.shard_map(
        functools.partial(body, mesh.shape["prow"], mesh.shape["pcol"]),
        mesh=mesh,
        in_specs=(
            P(None, None, ("prow", "pcol")),
            P(("prow", "pcol"), None),
            P(None, "prow", "pcol"),
            P(None, "prow"),
            P(None, "prow", None),
        ),
        out_specs=P(None, "prow", "pcol"),
        check_vma=False,
    )
```

```python
import functools

import jax
import jax.numpy as jnp
from jax import lax
from jax.experimental import pallas as pl
from jax.experimental.pallas import tpu as pltpu
from jax.sharding import PartitionSpec as P

MESH = pl.DeviceIdType.MESH
F32 = jnp.float32
BF16 = jnp.bfloat16


def split(value):
    high = value.astype(BF16)
    return high, (value - high.astype(F32)).astype(BF16)


def product(left_high, left_low, right_high, right_low):
    dot = functools.partial(jnp.dot, preferred_element_type=F32)
    small = dot(left_low, right_high) + dot(left_high, right_low)
    return small + dot(left_high, right_high)


def kernel(
    sizes, panel, solved, right_side, coupling, inverses, out,
    left, right, sent, received, own, x_u, y_v, y_u, x_v, z_last,
    side_cut, side, inv_got, inv_high, inv_low, coup_got, coup_high, coup_low,
    gathered, coupled, z_coupled, block_high, block_low, mine, theirs,
    side_s, side_r, iy_s, iy_r, ic_s, ic_r, cy_s, cy_r, cc_s, cc_r,
    core_s, core_r, xu_s, xu_r, yv_s, yv_r, yu_s, yu_r, xv_s, xv_r,
    zl_s, zl_r, g0_s, g0_r, zc_s, zc_r, g1_s, g1_r, end_s, end_r,
):
    A, B, X, K, tr, qr, cw = sizes
    half = cw // 2
    block = B * tr
    row, col = lax.axis_index("prow"), lax.axis_index("pcol")
    a, b = row // B, row % B
    x, c = col // 2, col % 2
    other_b, other_c = 1 - b, 1 - c

    def at(a_, b_, x_, c_):
        return (a_ * B + b_, x_ * 2 + c_)

    core_peer = at(a, b, x, other_c)
    y_peer = at(a, other_b, x, c)

    def x_peer(d):
        return at(a, b, lax.rem(x + d, X), c)

    def z_peer(d):
        return at(lax.rem(a + d, A), b, x, c)

    peers = [core_peer, y_peer]
    peers += [x_peer(d) for d in range(1, X)] + [z_peer(d) for d in range(1, A)]
    barrier = pltpu.get_barrier_semaphore()
    for peer in peers:
        pl.semaphore_signal(barrier, inc=1, device_id=peer, device_id_type=MESH)

    def copy(src, dst, s, r, peer):
        return pltpu.make_async_remote_copy(
            src_ref=src, dst_ref=dst, send_sem=s, recv_sem=r,
            device_id=peer, device_id_type=MESH,
        )

    for b_ in range(B):
        side_cut[b_] = right_side[:, :, b_ * half:(b_ + 1) * half]
    side[:, b] = side_cut[b]

    def split_right(q):
        high, low = split(solved[:, q * cw:(q + 1) * cw])
        right[q, 0:K] = high
        right[q, K:2 * K] = low
        right[q, 2 * K:] = high

    def split_left(t):
        for v in range(2):
            high, low = split(panel[t // 2, :, t % 2, v].reshape(A * qr, K))
            left[t, v, :, 0:K] = high
            left[t, v, :, K:2 * K] = high
            left[t, v, :, 2 * K:] = low

    pl.semaphore_wait(barrier, len(peers))

    def inverse_y(p):
        return copy(inverses.at[p, c], inv_got.at[p, c], iy_s.at[p], iy_r.at[p], y_peer)

    def inverse_core(p):
        return copy(inv_got.at[p, c], inv_got.at[p, c], ic_s.at[p], ic_r.at[p], core_peer)

    coupling_y = copy(coupling.at[c], coup_got.at[c], cy_s, cy_r, y_peer)
    coupling_core = copy(coup_got.at[c], coup_got.at[c], cc_s, cc_r, core_peer)
    side_y = copy(side_cut.at[other_b], side.at[:, b], side_s, side_r, y_peer)
    inverse_y(0).start()
    side_y.start()

    for q in range(2 * X):
        split_right(q)

    def multiply(t, q):
        lhs = left[t].reshape(2 * A * qr, 3 * K)
        return jnp.dot(lhs, right[q], preferred_element_type=F32).reshape(2, A, qr, cw)

    def core(t, x_):
        return copy(sent.at[t, x_], received.at[t, x_], core_s.at[t, x_], core_r.at[t, x_], core_peer)

    def compute(t):
        split_left(t)

        @pl.loop(0, X)
        def _(x_):
            value = multiply(t, x_ * 2 + other_c)
            for b_ in range(B):
                sent[t, x_, :, b_] = value[..., b_ * half:(b_ + 1) * half]
            core(t, x_).start()

        @pl.loop(0, X)
        def _(x_):
            value = multiply(t, x_ * 2 + c)
            core(t, x_).wait()
            for b_ in range(B):
                own[t, x_, :, b_] = value[..., b_ * half:(b_ + 1) * half] + received[t, x_, :, b_]

    def first_u(t):
        return [copy(own.at[t, lax.rem(x + d, X), 0], x_u.at[t, d - 1], xu_s.at[t, d - 1], xu_r.at[t, d - 1], x_peer(d)) for d in range(1, X)]

    def first_v(t):
        return [copy(own.at[t, :, 1, other_b], y_v.at[t], yv_s.at[t], yv_r.at[t], y_peer)]

    def second_u(t):
        return [copy(own.at[t, x, 0, other_b], y_u.at[t], yu_s.at[t], yu_r.at[t], y_peer)]

    def second_v(t):
        return [copy(own.at[t, lax.rem(x + d, X), 1, b], x_v.at[t, d - 1], xv_s.at[t, d - 1], xv_r.at[t, d - 1], x_peer(d)) for d in range(1, X)]

    def start(copies):
        for each in copies:
            each.start()

    def wait(copies):
        for each in copies:
            each.wait()

    def start_first(t):
        start(first_u(t))
        start(first_v(t))

    def turn(t):
        wait(first_u(t))
        for b_ in range(B):
            total = own[t, x, 0, b_]
            for d in range(1, X):
                total = total + x_u[t, d - 1, b_]
            own[t, x, 0, b_] = total
        start(second_u(t))
        wait(first_v(t))
        for x_ in range(X):
            own[t, x_, 1, b] = own[t, x_, 1, b] + y_v[t, x_]
        start(second_v(t))

    def finish(t):
        wait(second_u(t))
        own[t, x, 0, b] = own[t, x, 0, b] + y_u[t]
        wait(second_v(t))
        total = own[t, x, 1, b]
        for d in range(1, X):
            total = total + x_v[t, d - 1]
        own[t, x, 1, b] = total

    def along_z(t):
        return [copy(own.at[t, x, :, b, lax.rem(a + d, A)], z_last.at[t, d - 1], zl_s.at[t, d - 1], zl_r.at[t, d - 1], z_peer(d)) for d in range(1, A)]

    def gather_first(g):
        shard = gathered.at[0, a, g]
        return [copy(shard, shard, g0_s.at[g, d - 1], g0_r.at[g, d - 1], z_peer(d)) for d in range(1, A)]

    def rest(g):
        wait(along_z(g))
        for v in range(2):
            total = own[g, x, v, b, a]
            for d in range(1, A):
                total = total + z_last[g, d - 1, v]
            at_row = (g * 2 + v) * qr
            gathered[0, a, g, v * qr:(v + 1) * qr] = side[0, at_row // tr, at_row % tr:at_row % tr + qr] - total
        start(gather_first(g))

    def hold_inverse(p, b_, value):
        for a_ in range(A):
            high, low = split(value[:, a_ * block:(a_ + 1) * block])
            inv_high[p, a_, b_] = high
            inv_low[p, a_, b_] = low

    def got_inverse(p):
        inverse_core(p).wait()
        hold_inverse(p, other_b, inv_got[p].reshape(tr, A * block))

    def times_inverse(p, a_):
        high, low = split(gathered[p, a_].reshape(block, half))
        shape = (block, block)
        return product(inv_high[p, a_].reshape(shape), inv_low[p, a_].reshape(shape), high, low)

    compute(0)
    start_first(0)
    compute(1)
    turn(0)
    start_first(1)
    inverse_y(0).wait()
    inverse_core(0).start()
    compute(2)
    finish(0)
    start(along_z(0))
    turn(1)
    start_first(2)
    coupling_y.start()
    compute(3)
    finish(1)
    start(along_z(1))
    turn(2)
    start_first(3)
    side_y.wait()
    rest(0)
    hold_inverse(0, b, inverses[0].reshape(tr, A * block))
    got_inverse(0)
    rest(1)
    high, low = split(coupling[...].reshape(A, block, tr))
    coup_high[:, :, 0:tr] = high
    coup_low[:, :, 0:tr] = low
    coupling_y.wait()
    coupling_core.start()
    finish(2)
    turn(3)
    inverse_y(1).start()
    coupling_core.wait()
    high, low = split(coup_got[...].reshape(A, block, tr))
    coup_high[:, :, tr:] = high
    coup_low[:, :, tr:] = low
    hold_inverse(1, b, inverses[1].reshape(tr, A * block))

    first_panel = times_inverse(0, a)
    for d in range(1, A):
        for g in range(2):
            gather_first(g)[d - 1].wait()
        first_panel = first_panel + times_inverse(0, lax.rem(a + A - d, A))

    def finalize(p, value):
        mine[p] = value.reshape(B, tr, half)
        return copy(mine.at[p, other_b], theirs.at[p], end_s.at[p], end_r.at[p], y_peer)

    def result(p):
        ours, got = mine[p, b], theirs[p]
        out[p, :, 0:half] = jnp.where(b == 0, ours, got)
        out[p, :, half:] = jnp.where(b == 0, got, ours)

    end_first = finalize(0, first_panel)
    end_first.start()
    for each, ref in zip(split(first_panel.reshape(B, tr, half)), (block_high, block_low)):
        ref[...] = each
    finish(3)

    def ordered(ref):
        return jnp.concatenate([ref[b], ref[other_b]], axis=0)

    panel_high, panel_low = ordered(block_high), ordered(block_low)

    def coupled_z(d):
        return copy(coupled.at[lax.rem(a + d, A)], z_coupled.at[d - 1], zc_s.at[d - 1], zc_r.at[d - 1], z_peer(d))

    for d in list(range(1, A)) + [0]:
        a_ = lax.rem(a + d, A)
        value = product(coup_high[a_], coup_low[a_], panel_high, panel_low).reshape(2, 2, qr, half)
        for g in range(2):
            for v in range(2):
                coupled[a_, g, v] = value[g, v] + own[2 + g, x, v, b, a_]
        if d:
            coupled_z(d).start()
    inverse_y(1).wait()
    inverse_core(1).start()
    got_inverse(1)
    end_first.wait()
    result(0)
    total = coupled[a]
    for d in range(1, A):
        coupled_z(d).wait()
        total = total + z_coupled[d - 1]
    gathered[1, a] = (side[1].reshape(block, half) - total.reshape(block, half)).reshape(2, 2 * qr, half)
    shard = gathered.at[1, a]
    last = [copy(shard, shard, g1_s.at[d - 1], g1_r.at[d - 1], z_peer(d)) for d in range(1, A)]
    start(last)
    second_panel = times_inverse(1, a)
    for d in range(1, A):
        last[d - 1].wait()
        second_panel = second_panel + times_inverse(1, lax.rem(a + A - d, A))
    end_second = finalize(1, second_panel)
    end_second.start()
    end_second.wait()
    result(1)


def body(R, C, panel_rows, solved, right_side, coupling, inverses):
    B = 2
    A, X = R // B, C // 2
    K = panel_rows.shape[2]
    tr, cw = right_side.shape[1:]
    qr, half, block, rows = B * tr // 4, cw // 2, B * tr, R * tr
    vmem, dma = pltpu.VMEM, pltpu.SemaphoreType.DMA
    steps = [(), (2,), (2,), (), (), (4, X), (4, X - 1), (4,), (4,), (4, X - 1), (2, A - 1), (2, A - 1), (A - 1,), (A - 1,), (2,)]
    sems = []
    for shape in steps:
        sems += [dma(shape) if shape else dma, dma(shape) if shape else dma]
    return pl.pallas_call(
        functools.partial(kernel, (A, B, X, K, tr, qr, cw)),
        out_shape=jax.ShapeDtypeStruct((2, tr, cw), F32),
        in_specs=[pl.BlockSpec(memory_space=pltpu.VMEM)] * 5,
        out_specs=pl.BlockSpec(memory_space=pltpu.VMEM),
        scratch_shapes=[
            vmem((4, 2, A * qr, 3 * K), BF16),
            vmem((C, 3 * K, cw), BF16),
            vmem((4, X, 2, B, A, qr, half), F32),
            vmem((4, X, 2, B, A, qr, half), F32),
            vmem((4, X, 2, B, A, qr, half), F32),
            vmem((4, X - 1, B, A, qr, half), F32),
            vmem((4, X, A, qr, half), F32),
            vmem((4, A, qr, half), F32),
            vmem((4, X - 1, A, qr, half), F32),
            vmem((2, A - 1, 2, qr, half), F32),
            vmem((B, 2, tr, half), F32),
            vmem((2, B, tr, half), F32),
            vmem((2, 2, tr // 2, rows), F32),
            vmem((2, A, B, tr, block), BF16),
            vmem((2, A, B, tr, block), BF16),
            vmem((2, rows // 2, tr), F32),
            vmem((A, block, B * tr), BF16),
            vmem((A, block, B * tr), BF16),
            vmem((2, A, 2, 2 * qr, half), F32),
            vmem((A, 2, 2, qr, half), F32),
            vmem((A - 1, 2, 2, qr, half), F32),
            vmem((B, tr, half), BF16),
            vmem((B, tr, half), BF16),
            vmem((2, B, tr, half), F32),
            vmem((2, tr, half), F32),
        ] + sems,
        compiler_params=pltpu.CompilerParams(
            collective_id=0, has_side_effects=True, vmem_limit_bytes=58 << 20
        ),
    )(
        panel_rows.reshape(2, A, 2, 2, qr, K),
        solved,
        right_side,
        coupling.reshape(2, rows // 2, tr),
        inverses.reshape(2, 2, tr // 2, rows),
    )


def solution(mesh):
    return jax.shard_map(
        functools.partial(body, mesh.shape["prow"], mesh.shape["pcol"]),
        mesh=mesh,
        in_specs=(
            P(None, None, ("prow", "pcol")),
            P(("prow", "pcol"), None),
            P(None, "prow", "pcol"),
            P(None, "prow"),
            P(None, "prow", None),
        ),
        out_specs=P(None, "prow", "pcol"),
        check_vma=False,
    )
```

```python
import functools

import jax
import jax.numpy as jnp
from jax import lax
from jax.experimental import pallas as pl
from jax.experimental.pallas import tpu as pltpu
from jax.sharding import PartitionSpec as P

MESH = pl.DeviceIdType.MESH
F32 = jnp.float32
BF16 = jnp.bfloat16


def split(value):
    high = value.astype(BF16)
    return high, (value - high.astype(F32)).astype(BF16)


def product(left_high, left_low, right_high, right_low):
    dot = functools.partial(jnp.dot, preferred_element_type=F32)
    small = dot(left_low, right_high) + dot(left_high, right_low)
    return small + dot(left_high, right_high)


def kernel(
    sizes, panel_hbm, solved_hbm, right_side, coupling_hbm, inverses_hbm, out,
    panel, solved, coupling, inverses, in_sem,
    left, right, sent, received, own, x_u, y_v, y_u, x_v, z_last,
    inv_got, inv_high, inv_low, coup_got, coup_high, coup_low,
    gathered, coupled, z_coupled, block_high, block_low, mine, theirs,
    iy_s, iy_r, ix_s, ix_r, ic_s, ic_r, cy_s, cy_r, cx_s, cx_r, cc_s, cc_r,
    core_s, core_r, xu_s, xu_r, yv_s, yv_r, yu_s, yu_r, xv_s, xv_r,
    zl_s, zl_r, g0_s, g0_r, zc_s, zc_r, g1_s, g1_r, end_s, end_r,
):
    A, B, X, K, tr, qr, cw = sizes
    half = cw // 2
    block = B * tr
    width = A * block // (2 * X)
    row, col = lax.axis_index("prow"), lax.axis_index("pcol")
    a, b = row // B, row % B
    x, c = col // 2, col % 2
    other_b, other_c = 1 - b, 1 - c

    def at(a_, b_, x_, c_):
        return (a_ * B + b_, x_ * 2 + c_)

    core_peer = at(a, b, x, other_c)
    y_peer = at(a, other_b, x, c)

    def x_peer(d):
        return at(a, b, lax.rem(x + d, X), c)

    def z_peer(d):
        return at(lax.rem(a + d, A), b, x, c)

    def load(index, src, dst):
        return pltpu.make_async_copy(src, dst, in_sem.at[index])

    load_solved = load(0, solved_hbm, solved)
    load_panel = [load(1 + t, panel_hbm.at[t // 2, :, t % 2], panel.at[t]) for t in range(4)]
    load_inverses = load(5, inverses_hbm, inverses)
    load_coupling = load(6, coupling_hbm, coupling)
    for each in [load_solved] + load_panel + [load_inverses, load_coupling]:
        each.start()

    peers = [core_peer, y_peer]
    peers += [x_peer(d) for d in range(1, X)] + [z_peer(d) for d in range(1, A)]
    barrier = pltpu.get_barrier_semaphore()
    for peer in peers:
        pl.semaphore_signal(barrier, inc=1, device_id=peer, device_id_type=MESH)

    def copy(src, dst, s, r, peer):
        return pltpu.make_async_remote_copy(
            src_ref=src, dst_ref=dst, send_sem=s, recv_sem=r,
            device_id=peer, device_id_type=MESH,
        )

    def split_right(q):
        high, low = split(solved[:, q * cw:(q + 1) * cw])
        right[q, 0:K] = high
        right[q, K:2 * K] = low
        right[q, 2 * K:] = high

    def split_left(t):
        for v in range(2):
            high, low = split(panel[t, :, v].reshape(A * qr, K))
            left[t, v, :, 0:K] = high
            left[t, v, :, K:2 * K] = high
            left[t, v, :, 2 * K:] = low

    def columns(p):
        return inverses.at[p, :, pl.ds(pl.multiple_of(col * width, width), width)]

    def inverse_y(p):
        return copy(columns(p), inv_got.at[p, c, x], iy_s.at[p], iy_r.at[p], y_peer)

    def inverse_x(p, d):
        return copy(inv_got.at[p, c, x], inv_got.at[p, c, x], ix_s.at[p, d - 1], ix_r.at[p, d - 1], x_peer(d))

    def inverse_core(p):
        return copy(inv_got.at[p, c], inv_got.at[p, c], ic_s.at[p], ic_r.at[p], core_peer)

    def coupling_x(d):
        return copy(coup_got.at[c, x], coup_got.at[c, x], cx_s.at[d - 1], cx_r.at[d - 1], x_peer(d))

    coupling_y = copy(coupling.at[x, c], coup_got.at[c, x], cy_s, cy_r, y_peer)
    coupling_core = copy(coup_got.at[c], coup_got.at[c], cc_s, cc_r, core_peer)
    load_solved.wait()
    for q in range(2 * X):
        split_right(q)

    def multiply(t, q):
        lhs = left[t].reshape(2 * A * qr, 3 * K)
        return jnp.dot(lhs, right[q], preferred_element_type=F32).reshape(2, A, qr, cw)

    def core(t, x_):
        return copy(sent.at[t, x_], received.at[t, x_], core_s.at[t, x_], core_r.at[t, x_], core_peer)

    def compute(t):
        load_panel[t].wait()
        split_left(t)
        if t == 0:
            pl.semaphore_wait(barrier, len(peers))

        @pl.loop(0, X)
        def _(x_):
            value = multiply(t, x_ * 2 + other_c)
            for b_ in range(B):
                sent[t, x_, :, b_] = value[..., b_ * half:(b_ + 1) * half]
            core(t, x_).start()

        @pl.loop(0, X)
        def _(x_):
            value = multiply(t, x_ * 2 + c)
            core(t, x_).wait()
            for b_ in range(B):
                own[t, x_, :, b_] = value[..., b_ * half:(b_ + 1) * half] + received[t, x_, :, b_]

        for v in range(2):
            for b_ in range(B):
                ours = right_side[t // 2, v * qr:(v + 1) * qr, b_ * half:(b_ + 1) * half]
                ours = jnp.where(b == t % 2, ours, jnp.zeros_like(ours))
                own[t, x, v, b_, a] = own[t, x, v, b_, a] - ours

    def first_u(t):
        return [copy(own.at[t, lax.rem(x + d, X), 0], x_u.at[t, d - 1], xu_s.at[t, d - 1], xu_r.at[t, d - 1], x_peer(d)) for d in range(1, X)]

    def first_v(t):
        return [copy(own.at[t, :, 1, other_b], y_v.at[t], yv_s.at[t], yv_r.at[t], y_peer)]

    def second_u(t):
        return [copy(own.at[t, x, 0, other_b], y_u.at[t], yu_s.at[t], yu_r.at[t], y_peer)]

    def second_v(t):
        return [copy(own.at[t, lax.rem(x + d, X), 1, b], x_v.at[t, d - 1], xv_s.at[t, d - 1], xv_r.at[t, d - 1], x_peer(d)) for d in range(1, X)]

    def start(copies):
        for each in copies:
            each.start()

    def wait(copies):
        for each in copies:
            each.wait()

    def start_first(t):
        start(first_u(t))
        start(first_v(t))

    def turn(t):
        wait(first_u(t))
        for b_ in range(B):
            total = own[t, x, 0, b_]
            for d in range(1, X):
                total = total + x_u[t, d - 1, b_]
            own[t, x, 0, b_] = total
        start(second_u(t))
        wait(first_v(t))
        for x_ in range(X):
            own[t, x_, 1, b] = own[t, x_, 1, b] + y_v[t, x_]
        start(second_v(t))

    def finish(t):
        wait(second_u(t))
        own[t, x, 0, b] = own[t, x, 0, b] + y_u[t]
        wait(second_v(t))
        total = own[t, x, 1, b]
        for d in range(1, X):
            total = total + x_v[t, d - 1]
        own[t, x, 1, b] = total

    def along_z(t):
        return [copy(own.at[t, x, :, b, lax.rem(a + d, A)], z_last.at[t, d - 1], zl_s.at[t, d - 1], zl_r.at[t, d - 1], z_peer(d)) for d in range(1, A)]

    def gather_first(g, d):
        shard = gathered.at[0, a, g]
        return copy(shard, shard, g0_s.at[g, d - 1], g0_r.at[g, d - 1], z_peer(d))

    def rest(g):
        wait(along_z(g))
        for v in range(2):
            total = own[g, x, v, b, a]
            for d in range(1, A):
                total = total + z_last[g, d - 1, v]
            gathered[0, a, g, v * qr:(v + 1) * qr] = -total
        for d in range(1, A):
            gather_first(g, d).start()

    def hold_inverse(p, b_, value):
        for a_ in range(A):
            high, low = split(value[:, a_ * block:(a_ + 1) * block])
            inv_high[p, a_, b_] = high
            inv_low[p, a_, b_] = low

    def got_inverse(p):
        inverse_core(p).wait()
        for a_ in range(A):
            piece, offset = a_ * block // width, a_ * block % width
            high, low = split(inv_got[p, piece % 2, piece // 2, :, offset:offset + block])
            inv_high[p, a_, other_b] = high
            inv_low[p, a_, other_b] = low

    def times_inverse(p, a_):
        high, low = split(gathered[p, a_].reshape(block, half))
        shape = (block, block)
        return product(inv_high[p, a_].reshape(shape), inv_low[p, a_].reshape(shape), high, low)

    compute(0)
    start_first(0)
    compute(1)
    turn(0)
    start_first(1)
    compute(2)
    finish(0)
    start(along_z(0))
    turn(1)
    start_first(2)
    load_inverses.wait()
    load_coupling.wait()
    inverse_y(0).start()
    coupling_y.start()
    compute(3)
    finish(1)
    start(along_z(1))
    rest(0)
    turn(2)
    start_first(3)
    hold_inverse(0, b, inverses[0])
    inverse_y(0).wait()
    for d in range(1, X):
        inverse_x(0, d).start()
    coupling_y.wait()
    for d in range(1, X):
        coupling_x(d).start()
    rest(1)
    high, low = split(coupling[...].reshape(A, block, tr))
    coup_high[:, :, 0:tr] = high
    coup_low[:, :, 0:tr] = low
    finish(2)
    turn(3)
    inverse_y(1).start()
    for d in range(1, X):
        inverse_x(0, d).wait()
    inverse_core(0).start()
    for d in range(1, X):
        coupling_x(d).wait()
    coupling_core.start()
    hold_inverse(1, b, inverses[1])
    got_inverse(0)
    coupling_core.wait()
    many = width // block
    for q in range(2 * X):
        high, low = split(coup_got[q % 2, q // 2].reshape(many, block, tr))
        coup_high[q * many:(q + 1) * many, :, tr:] = high
        coup_low[q * many:(q + 1) * many, :, tr:] = low

    first_panel = times_inverse(0, a)
    for d in range(1, A):
        for g in range(2):
            gather_first(g, d).wait()
        first_panel = first_panel + times_inverse(0, lax.rem(a + A - d, A))

    def finalize(p, value):
        mine[p] = value.reshape(B, tr, half)
        return copy(mine.at[p, other_b], theirs.at[p], end_s.at[p], end_r.at[p], y_peer)

    def result(p):
        ours, got = mine[p, b], theirs[p]
        out[p, :, 0:half] = jnp.where(b == 0, ours, got)
        out[p, :, half:] = jnp.where(b == 0, got, ours)

    end_first = finalize(0, first_panel)
    end_first.start()
    inverse_y(1).wait()
    for d in range(1, X):
        inverse_x(1, d).start()
    for each, ref in zip(split(first_panel.reshape(B, tr, half)), (block_high, block_low)):
        ref[...] = each
    finish(3)

    def ordered(ref):
        return jnp.concatenate([ref[b], ref[other_b]], axis=0)

    panel_high, panel_low = ordered(block_high), ordered(block_low)

    def coupled_z(d):
        return copy(coupled.at[lax.rem(a + d, A)], z_coupled.at[d - 1], zc_s.at[d - 1], zc_r.at[d - 1], z_peer(d))

    for d in list(range(1, A)) + [0]:
        a_ = lax.rem(a + d, A)
        value = product(coup_high[a_], coup_low[a_], panel_high, panel_low).reshape(2, 2, qr, half)
        for g in range(2):
            for v in range(2):
                coupled[a_, g, v] = value[g, v] + own[2 + g, x, v, b, a_]
        if d:
            coupled_z(d).start()
    for d in range(1, X):
        inverse_x(1, d).wait()
    inverse_core(1).start()
    got_inverse(1)
    end_first.wait()
    result(0)
    total = coupled[a]
    for d in range(1, A):
        coupled_z(d).wait()
        total = total + z_coupled[d - 1]
    gathered[1, a] = -total.reshape(2, 2 * qr, half)

    def hop(held, step):
        block_ref = gathered.at[1, lax.rem(a + A - held, A)]
        return copy(block_ref, block_ref, g1_s.at[step], g1_r.at[step], z_peer(1))

    @pl.when(a < A - 1)
    def _():
        hop(0, 0).start()

    mine[1] = times_inverse(1, a).reshape(B, tr, half)
    for step in range(1, A):

        @pl.when(a >= step)
        def _():
            hop(step, step - 1).wait_recv()
            if step < A - 1:

                @pl.when(a < A - 1)
                def _():
                    hop(step, step).start()

            mine[1] = mine[1] + times_inverse(1, lax.rem(a + A - step, A)).reshape(B, tr, half)

    for step in range(A - 1):

        @pl.when((a < A - 1) & (a >= step))
        def _():
            hop(step, step).wait_send()

    second_panel = mine[1]
    end_second = finalize(1, second_panel)
    end_second.start()
    end_second.wait()
    result(1)


def body(R, C, panel_rows, solved, right_side, coupling, inverses):
    B = 2
    A, X = R // B, C // 2
    K = panel_rows.shape[2]
    tr, cw = right_side.shape[1:]
    qr, half, block, rows = B * tr // 4, cw // 2, B * tr, R * tr
    vmem, dma = pltpu.VMEM, pltpu.SemaphoreType.DMA
    steps = [(2,), (2, X - 1), (2,), (), (X - 1,), (), (4, X), (4, X - 1), (4,), (4,), (4, X - 1), (2, A - 1), (2, A - 1), (A - 1,), (A - 1,), (2,)]
    sems = []
    for shape in steps:
        sems += [dma(shape) if shape else dma, dma(shape) if shape else dma]
    return pl.pallas_call(
        functools.partial(kernel, (A, B, X, K, tr, qr, cw)),
        out_shape=jax.ShapeDtypeStruct((2, tr, cw), F32),
        in_specs=[pl.BlockSpec(memory_space=pltpu.VMEM if i == 2 else pl.ANY) for i in range(5)],
        out_specs=pl.BlockSpec(memory_space=pltpu.VMEM),
        scratch_shapes=[
            vmem((4, A, 2, qr, K), F32),
            vmem((K, C * cw), F32),
            vmem((X, 2, rows // C, tr), F32),
            vmem((2, tr, rows), F32),
            dma((7,)),
            vmem((4, 2, A * qr, 3 * K), BF16),
            vmem((C, 3 * K, cw), BF16),
            vmem((4, X, 2, B, A, qr, half), F32),
            vmem((4, X, 2, B, A, qr, half), F32),
            vmem((4, X, 2, B, A, qr, half), F32),
            vmem((4, X - 1, B, A, qr, half), F32),
            vmem((4, X, A, qr, half), F32),
            vmem((4, A, qr, half), F32),
            vmem((4, X - 1, A, qr, half), F32),
            vmem((2, A - 1, 2, qr, half), F32),
            vmem((2, 2, X, tr, rows // C), F32),
            vmem((2, A, B, tr, block), BF16),
            vmem((2, A, B, tr, block), BF16),
            vmem((2, X, rows // C, tr), F32),
            vmem((A, block, B * tr), BF16),
            vmem((A, block, B * tr), BF16),
            vmem((2, A, 2, 2 * qr, half), F32),
            vmem((A, 2, 2, qr, half), F32),
            vmem((A - 1, 2, 2, qr, half), F32),
            vmem((B, tr, half), BF16),
            vmem((B, tr, half), BF16),
            vmem((2, B, tr, half), F32),
            vmem((2, tr, half), F32),
        ] + sems,
        compiler_params=pltpu.CompilerParams(
            collective_id=0, has_side_effects=True, vmem_limit_bytes=58 << 20
        ),
    )(
        panel_rows.reshape(2, A, 2, 2, qr, K),
        solved,
        right_side,
        coupling.reshape(X, 2, rows // C, tr),
        inverses,
    )


def solution(mesh):
    return jax.shard_map(
        functools.partial(body, mesh.shape["prow"], mesh.shape["pcol"]),
        mesh=mesh,
        in_specs=(
            P(None, None, ("prow", "pcol")),
            P(("prow", "pcol"), None),
            P(None, "prow", "pcol"),
            P(None, "prow"),
            P(None, "prow", None),
        ),
        out_specs=P(None, "prow", "pcol"),
        check_vma=False,
    )
```
